32 devices in a mesh: mp: 2 (over x), lat: 8 (over z, y), lon: 2 (over core).
Axes of the slice: x: 2, y: 2, z: 4, core: 2. Of those that a mesh axis runs over, the one named last changes fastest.
Arguments:
- state: bfloat16 [2, 160, 128, 1536], P('mp', None, 'lat', 'lon'), may hold values from -6 to 6
- conv_first: bfloat16 [2, 3, 3, 160, 160], P('mp'), may hold values from -0.15625 to 0.15625
- bias_first: float32 [2, 160], P('mp'), may hold values from -3 to 3
- conv_second: bfloat16 [2, 3, 3, 160, 160], P('mp'), may hold values from -0.15625 to 0.15625
- bias_second: float32 [2, 160], P('mp'), may hold values from -3 to 3
- norm_gain: float32 [2, 160], P('mp'), may hold values from 0.1 to 1.9
- export_weight: bfloat16 [2, 160, 8], P('mp'), may hold values from -0.5 to 0.5
- import_weight: bfloat16 [2, 8, 160], P('mp'), may hold values from -2 to 2
- regrid_rows: int32 [2, 128, 4], P('mp', 'lat'), may hold values from 0 to 127, as said below
- regrid_weights: float32 [2, 128, 4], P('mp', 'lat'), may hold values from 0.2 to 1
- sea_mask: int32 [2, 128, 1536], P('mp', 'lat', 'lon'), may hold values 0 or 1
Outputs:
- coupled: bfloat16 [2, 160, 128, 1536], P('mp', None, 'lat', 'lon')
The draws below stay inside these ranges and needn't reach their ends.
Inputs may be any that keep to these rules, and one draw needn't show every extreme that they name: `regrid_rows`: the source rows of destination row d lie within 16 rows of d, and the first of them is row d itself.
All inputs are finite; a program needn't handle non-finite values. No bound on the sum of `sea_mask` on one device may be relied on, other than what follows from the above.
Results may differ from the reference program's by a relative error of at most 0.0065.
Values may be sent and summed in bfloat16 or wider, within the bound.
A program may use at most 192 MiB of HBM per device.

```python
import jax
import jax.numpy as jnp
from jax import lax

CH = 160
NI = 8
SOURCES = 4
R_DEV = 16
NLAT = 128
NLON = 1536


def draw_regrid_rows(key, part):
    key = jax.random.fold_in(key, 17)
    shifts = jax.random.randint(key, (2, NLAT, SOURCES), -R_DEV, R_DEV + 1)
    leading = jnp.arange(SOURCES, dtype=jnp.int32)[None, None, :] == 0
    shifts = jnp.where(leading, 0, shifts)
    row_index = jnp.arange(NLAT, dtype=jnp.int32)[None, :, None]
    return jnp.clip(row_index + shifts, 0, NLAT - 1).astype(jnp.int32)


def set_ends(entries, stream_key, low, top_value):
    index_at = [jax.random.randint(jax.random.fold_in(stream_key, axis), (), 0, length) for axis, length in enumerate(entries.shape)]
    longest = entries.shape.index(max(entries.shape))
    beside = index_at[:longest] + [(index_at[longest] + 1) % entries.shape[longest]] + index_at[longest + 1:]
    return entries.at[tuple(index_at)].set(low).at[tuple(beside)].set(top_value)


def shard_levels(rng, dims, cuts, smallest, largest):
    def one(axis_at, parts):
        heights = jax.random.uniform(jax.random.fold_in(jax.random.fold_in(rng, 6), axis_at), (parts,), jnp.float32, smallest / len(cuts), largest / len(cuts))
        return jnp.repeat(jnp.exp(heights), dims[axis_at] // parts).reshape((-1,) + (1,) * (len(dims) - axis_at - 1))

    gain = one(*cuts[0])
    for cut in cuts[1:]:
        gain = gain * one(*cut)
    return gain


def noise(key, shape, spread, most, pieces=(), kind=jnp.bfloat16):
    gain = shard_levels(key, shape, pieces, -0.22, 0.18) if pieces else 1.0
    array = jax.random.normal(key, shape, jnp.float32) * spread * gain
    return jnp.minimum(jnp.maximum(array, -most), most).astype(kind)


def setup_inputs(seed: int = 0) -> dict:
    keys = jax.random.split(jax.random.key(seed), 12)
    state = noise(keys[0], (2, CH, NLAT, NLON), 1.0, 6.0, ((0, 2), (2, 8), (3, 2)))
    conv_first = noise(keys[1], (2, 3, 3, CH, CH), (9 * CH) ** -0.5, 0.15625, ((0, 2),))
    bias_first = noise(keys[2], (2, CH), 0.5, 3.0, ((0, 2),), jnp.float32)
    conv_second = noise(keys[3], (2, 3, 3, CH, CH), (9 * CH) ** -0.5, 0.15625, ((0, 2),))
    bias_second = noise(keys[4], (2, CH), 0.5, 3.0, ((0, 2),), jnp.float32)
    norm_gain = jnp.clip(1.0 + 0.18 * jax.random.normal(keys[5], (2, CH), jnp.float32), 0.1, 1.9)
    export_weight = noise(keys[6], (2, CH, NI), CH ** -0.5, 0.5, ((0, 2),))
    import_weight = noise(keys[7], (2, NI, CH), NI ** -0.5, 2.0, ((0, 2),))
    regrid_rows = draw_regrid_rows(jax.random.fold_in(keys[11], 71), 0)
    regrid_weights = jnp.clip(0.2 + 0.8 * jax.random.uniform(keys[9], (2, NLAT, SOURCES), jnp.float32) ** shard_levels(keys[9], (2, NLAT, SOURCES), ((0, 2), (1, 8)), -0.2, 0.2), 0.2, 1.0)
    sea_mask = set_ends((jax.random.randint(keys[10], (2, NLAT, NLON), 0, 10) < 7).astype(jnp.int32), jax.random.fold_in(keys[10], 1), 0, 1)
    return {"state": state, "conv_first": conv_first, "bias_first": bias_first, "conv_second": conv_second, "bias_second": bias_second, "norm_gain": norm_gain, "export_weight": export_weight, "import_weight": import_weight, "regrid_rows": regrid_rows, "regrid_weights": regrid_weights, "sea_mask": sea_mask}


def periodic_pad(source):
    padded = jnp.pad(source, ((0, 0), (1, 1), (0, 0)))
    return jnp.concatenate([padded[:, :, -1:], padded, padded[:, :, :1]], axis=2)

def convolve(source, kernel, offset):
    result = lax.conv_general_dilated(source[None], kernel, (1, 1), 'VALID', dimension_numbers=('NCHW', 'HWIO', 'NCHW'), preferred_element_type=jnp.float32)[0]
    return result + offset[:, None, None]

def reference(state, conv_first, bias_first, conv_second, bias_second, norm_gain, export_weight, import_weight, regrid_rows, regrid_weights, sea_mask):
    hidden_list = []
    face_list = []
    for section in range(2):
        source = state[section]
        hidden_first = jax.nn.silu(convolve(periodic_pad(source), conv_first[section], bias_first[section])).astype(jnp.bfloat16)
        before_norm = source.astype(jnp.float32) + convolve(periodic_pad(hidden_first), conv_second[section], bias_second[section])
        square_mean = lax.optimization_barrier(jnp.mean(before_norm * before_norm, axis=0, keepdims=True))
        hidden = (before_norm * lax.rsqrt(square_mean + 1e-06) * norm_gain[section][:, None, None]).astype(jnp.bfloat16)
        face_rows = jnp.einsum('cn,crl->nrl', export_weight[section].astype(jnp.float32), hidden.astype(jnp.float32), precision=lax.Precision.HIGHEST).astype(jnp.bfloat16)
        hidden_list.append(hidden)
        face_list.append(face_rows)
    outputs = []
    for section in range(2):
        other_rows = face_list[1 - section]
        gathered = jnp.take(other_rows, regrid_rows[section], axis=1)
        weights = regrid_weights[section]
        normed = weights / lax.optimization_barrier(jnp.sum(weights, axis=1, keepdims=True))
        arriving = jnp.einsum('nrkl,rk->nrl', gathered.astype(jnp.float32), normed, precision=lax.Precision.HIGHEST).astype(jnp.bfloat16)
        mixed_term = jnp.einsum('nc,nrl->crl', import_weight[section].astype(jnp.float32), arriving.astype(jnp.float32), precision=lax.Precision.HIGHEST)
        coupled = hidden_list[section].astype(jnp.float32) + sea_mask[section].astype(jnp.float32)[None] * mixed_term
        outputs.append(coupled.astype(jnp.bfloat16))
    return jnp.stack(outputs)
```

```python
import functools

import jax
import jax.numpy as jnp
from jax import lax
from jax.experimental import pallas as pl
from jax.experimental.pallas import tpu as pltpu
from jax.sharding import PartitionSpec as P

F32 = jnp.float32
BF16 = jnp.bfloat16
LANES = 128
SIDE = 64
VMEM_LIMIT = 58 * 1024 * 1024


def lane_of(shape):
    return lax.broadcasted_iota(jnp.int32, shape, 1)


def stacked_rows(edge):
    return jnp.concatenate(
        [pltpu.roll(edge, 1, 1), edge, pltpu.roll(edge, LANES - 1, 1)], axis=0
    ).astype(BF16)


def edge_terms(weights, edge):
    ch = edge.shape[0]
    taps = jnp.dot(weights, stacked_rows(edge), preferred_element_type=F32)
    return jnp.where(lane_of((ch, LANES)) < SIDE, taps[:ch], taps[2 * ch :])


def conv_row(weights, rows3, edges, row, offset):
    ch, width = edges.shape[0], rows3.shape[1]
    taps = jnp.dot(weights, rows3, preferred_element_type=F32)
    at = lane_of((ch, LANES))
    left = jnp.sum(jnp.where(at == row + 2, edges, 0.0), axis=1, keepdims=True)
    right = jnp.sum(jnp.where(at == row + 2 + SIDE, edges, 0.0), axis=1, keepdims=True)
    lane = lane_of((ch, width))
    west = jnp.where(lane == 0, left, pltpu.roll(taps[:ch], 1, 1))
    east = jnp.where(lane == width - 1, right, pltpu.roll(taps[2 * ch :], width - 1, 1))
    return taps[ch : 2 * ch] + west + east + offset


def silu(u):
    return u / (1.0 + jnp.exp(-u))


def first_kernel(x_ref, w_ref, b_ref, e_ref, xr_ref, hf_ref, flat, edges):
    ch, rows, width = x_ref.shape
    for j in range(width // LANES):
        flat[j] = x_ref[:, :, j * LANES : (j + 1) * LANES].astype(F32).reshape(ch * rows, LANES)
    for r in range(rows):
        for j in range(width // LANES):
            xr_ref[r * ch : (r + 1) * ch, j * LANES : (j + 1) * LANES] = flat.at[j][
                pl.ds(r, ch, stride=rows), :
            ].astype(BF16)
    edges[...] = edge_terms(w_ref[...], e_ref[...])

    @pl.loop(1, rows - 1)
    def _(r):
        rows3 = xr_ref[pl.ds(pl.multiple_of((r - 1) * ch, 16), 3 * ch), :]
        u = conv_row(w_ref[...], rows3, edges[...], r, b_ref[...])
        hf_ref[pl.ds(pl.multiple_of((r - 1) * ch, 16), ch), :] = silu(u).astype(BF16)


def second_kernel(
    ok_ref, xr_ref, top_ref, bot_ref, hf_ref, w1_ref, b1_ref, e_ref, w2_ref, b2_ref, g_ref,
    ex_ref, hid_ref, face_ref, xe, hfe, edges1, edges2,
):
    ch = g_ref.shape[0]
    width = xr_ref.shape[1]
    rows = xr_ref.shape[0] // ch
    xe[0, : 2 * ch] = top_ref[...]
    xe[0, 2 * ch :] = xr_ref[: 2 * ch]
    xe[1, : 2 * ch] = xr_ref[(rows - 2) * ch :]
    xe[1, 2 * ch :] = bot_ref[...]
    hfe[0, 2 * ch :] = hf_ref[: 2 * ch]
    hfe[1, : 2 * ch] = hf_ref[(rows - 4) * ch :]

    edges1[...] = edge_terms(w1_ref[...], e_ref[ch : 2 * ch])
    column = None
    for k in range(3):
        term = jnp.dot(
            w1_ref[k * ch : (k + 1) * ch],
            stacked_rows(e_ref[k * ch : (k + 1) * ch]),
            preferred_element_type=F32,
        )
        column = term if column is None else column + term
    column = silu(column + b1_ref[...])
    lane = lane_of((ch, LANES))
    lane = jnp.where(lane >= SIDE, lane - SIDE, lane)
    column = jnp.where((lane == 1) & (ok_ref[0] == 0), 0.0, column)
    column = jnp.where((lane == rows + 2) & (ok_ref[1] == 0), 0.0, column)
    column = jnp.where((lane < 1) | (lane > rows + 2), 0.0, column)
    edges2[...] = edge_terms(w2_ref[...], column.astype(BF16).astype(F32))

    @pl.loop(0, 4)
    def _(q):
        side, k = q // 2, q % 2
        rows3 = xe[side, pl.ds(pl.multiple_of(k * ch, 16), 3 * ch), :]
        r = jnp.where(side == 0, k - 1, rows - 1 + k)
        u = silu(conv_row(w1_ref[...], rows3, edges1[...], r, b1_ref[...]))
        gone = ((r < 0) & (ok_ref[0] == 0)) | ((r >= rows) & (ok_ref[1] == 0))
        u = jnp.where(gone, 0.0, u)
        hfe[side, pl.ds(pl.multiple_of((k + 2 * side) * ch, 16), ch), :] = u.astype(BF16)

    def finish(rows3, r):
        here = pl.ds(pl.multiple_of(r * ch, 16), ch)
        u = conv_row(w2_ref[...], rows3, edges2[...], r, b2_ref[...])
        u = u + xr_ref[here, :].astype(F32)
        mean = jnp.sum(u * u, axis=0, keepdims=True) * (1.0 / ch)
        h = (u * lax.rsqrt(mean + 1e-06) * g_ref[...]).astype(BF16)
        hid_ref[here, :] = h
        face_ref[r] = jnp.dot(ex_ref[...], h, preferred_element_type=F32).astype(BF16)

    @pl.loop(0, 4)
    def _(q):
        side, k = q // 2, q % 2
        rows3 = hfe[side, pl.ds(pl.multiple_of(k * ch, 16), 3 * ch), :]
        finish(rows3, jnp.where(side == 0, k, rows - 2 + k))

    @pl.loop(2, rows - 2)
    def _(r):
        finish(hf_ref[pl.ds(pl.multiple_of((r - 2) * ch, 16), 3 * ch), :], r)


def third_kernel(
    rows_ref, weights_ref, hid_ref, up_ref, mid_ref, down_ref, im_ref, mask_ref, out_ref, band, flat
):
    ch, step, width = out_ref.shape
    rows = up_ref.shape[0]
    base = pl.program_id(0) * step
    band[:rows] = up_ref[...].astype(F32)
    band[rows : 2 * rows] = mid_ref[...].astype(F32)
    band[2 * rows :] = down_ref[...].astype(F32)
    for d in range(step):
        total = None
        for k in range(rows_ref.shape[1]):
            term = weights_ref[base + d, k] * band[rows_ref[base + d, k]]
            total = term if total is None else total + term
        mixed = jnp.dot(im_ref[...], total.astype(BF16), preferred_element_type=F32)
        h = hid_ref[d * ch : (d + 1) * ch, :].astype(F32)
        value = h + mask_ref[d : d + 1, :].astype(F32) * mixed
        for j in range(width // LANES):
            flat.at[j][pl.ds(d, ch, stride=step), :] = value[:, j * LANES : (j + 1) * LANES]
    for j in range(width // LANES):
        out_ref[:, :, j * LANES : (j + 1) * LANES] = (
            flat[j].reshape(ch, step, LANES).astype(BF16)
        )


def vmem():
    return pl.BlockSpec(memory_space=pltpu.VMEM)


def smem():
    return pl.BlockSpec(memory_space=pltpu.SMEM)


def params():
    return pltpu.CompilerParams(vmem_limit_bytes=VMEM_LIMIT)


def both_ways(tail, head, axis):
    n = lax.axis_size(axis)
    return (
        lax.ppermute(tail, axis, [(i, i + 1) for i in range(n - 1)]),
        lax.ppermute(head, axis, [(i + 1, i) for i in range(n - 1)]),
    )


def on_device(
    state, conv_first, bias_first, conv_second, bias_second, norm_gain, export_weight,
    import_weight, regrid_rows, regrid_weights, sea_mask,
):
    source = state[0]
    ch, rows, width = source.shape
    lat = lax.axis_index("lat")
    n_lat = lax.axis_size("lat")

    def row_block(part):
        return part.transpose(1, 0, 2).reshape(-1, width)

    top, bot = both_ways(
        row_block(source[:, rows - 2 :]), row_block(source[:, :2]), "lat"
    )
    own = jnp.stack([source[:, :, i] for i in (0, 1, width - 2, width - 1)])
    far = lax.ppermute(own, "lon", [(0, 1), (1, 0)])
    cols = jnp.concatenate([far[2:4], own[0:1], own[3:4], far[0:2]])
    above, below = both_ways(cols[:, :, rows - 2 :], cols[:, :, :2], "lat")

    def in_lanes(cols, first_row):
        before = first_row + 2
        cols = jnp.pad(cols, ((0, 0), (0, 0), (before, SIDE - before - cols.shape[2])))
        return jnp.concatenate([cols[:3], cols[3:]], axis=2).reshape(3 * ch, LANES).astype(F32)

    edge_own = in_lanes(cols, 0)[ch : 2 * ch]
    edge_all = in_lanes(jnp.concatenate([above, cols, below], axis=2), -2)

    def taps(kernel):
        return kernel.transpose(1, 3, 0, 2).reshape(3 * ch, 3 * ch)

    w1, w2 = taps(conv_first[0]), taps(conv_second[0])
    b1, b2, gain = bias_first[0][:, None], bias_second[0][:, None], norm_gain[0][:, None]

    per_row = 2 * 9 * ch * ch * width
    xr, hf = pl.pallas_call(
        first_kernel,
        name="conv_first_inner",
        out_shape=(
            jax.ShapeDtypeStruct((rows * ch, width), BF16),
            jax.ShapeDtypeStruct(((rows - 2) * ch, width), BF16),
        ),
        in_specs=[vmem()] * 4,
        out_specs=(vmem(), vmem()),
        scratch_shapes=[
            pltpu.VMEM((width // LANES, rows * ch, LANES), F32),
            pltpu.VMEM((ch, LANES), F32),
        ],
        compiler_params=params(),
        cost_estimate=pl.CostEstimate(
            flops=per_row * (rows - 2), bytes_accessed=6 * rows * ch * width, transcendentals=0
        ),
    )(source, w1, b1, edge_own)

    ok = jnp.stack([lat > 0, lat < n_lat - 1]).astype(jnp.int32)
    n_face = export_weight.shape[2]
    hidden, face = pl.pallas_call(
        second_kernel,
        name="conv_second",
        out_shape=(
            jax.ShapeDtypeStruct((rows * ch, width), BF16),
            jax.ShapeDtypeStruct((rows, n_face, width), BF16),
        ),
        in_specs=[smem()] + [vmem()] * 11,
        out_specs=(vmem(), vmem()),
        scratch_shapes=[
            pltpu.VMEM((2, 4 * ch, width), BF16),
            pltpu.VMEM((2, 4 * ch, width), BF16),
            pltpu.VMEM((ch, LANES), F32),
            pltpu.VMEM((ch, LANES), F32),
        ],
        compiler_params=params(),
        cost_estimate=pl.CostEstimate(
            flops=per_row * (rows + 4), bytes_accessed=6 * rows * ch * width, transcendentals=0
        ),
    )(ok, xr, top, bot, hf, w1, b1, edge_all, w2, b2, gain, export_weight[0].T)

    mid = lax.ppermute(face, "mp", [(0, 1), (1, 0)])
    up, down = both_ways(mid, mid, "lat")
    weights = regrid_weights[0]
    normed = weights / jnp.sum(weights, axis=1, keepdims=True)
    local_rows = regrid_rows[0] - (lat - 1) * rows

    step = 8
    whole = lambda shape: pl.BlockSpec(shape, lambda i: (0,) * len(shape))
    out = pl.pallas_call(
        third_kernel,
        name="exchange",
        grid=(rows // step,),
        out_shape=jax.ShapeDtypeStruct((ch, rows, width), BF16),
        in_specs=[
            smem(),
            smem(),
            pl.BlockSpec((step * ch, width), lambda i: (i, 0)),
            whole(mid.shape),
            whole(mid.shape),
            whole(mid.shape),
            whole((ch, n_face)),
            pl.BlockSpec((step, width), lambda i: (i, 0)),
        ],
        out_specs=pl.BlockSpec((ch, step, width), lambda i: (0, i, 0)),
        scratch_shapes=[
            pltpu.VMEM((3 * rows, n_face, width), F32),
            pltpu.VMEM((width // LANES, step * ch, LANES), F32),
        ],
        compiler_params=params(),
    )(local_rows, normed, hidden, up, mid, down, import_weight[0].T, sea_mask[0])
    return out[None]


def solution(mesh):
    return jax.shard_map(
        on_device,
        mesh=mesh,
        in_specs=(
            P("mp", None, "lat", "lon"),
            P("mp", None, None, None, None),
            P("mp", None),
            P("mp", None, None, None, None),
            P("mp", None),
            P("mp", None),
            P("mp", None, None),
            P("mp", None, None),
            P("mp", "lat", None),
            P("mp", "lat", None),
            P("mp", "lat", "lon"),
        ),
        out_specs=P("mp", None, "lat", "lon"),
        check_vma=False,
    )
```

```python
import functools

import jax
import jax.numpy as jnp
from jax import lax
from jax.experimental import pallas as pl
from jax.experimental.pallas import tpu as pltpu
from jax.sharding import PartitionSpec as P

F32 = jnp.float32
BF16 = jnp.bfloat16
LANES = 128
SIDE = 64
VMEM_LIMIT = 58 * 1024 * 1024


def lane_of(shape):
    return lax.broadcasted_iota(jnp.int32, shape, 1)


def stacked_rows(edge):
    return jnp.concatenate(
        [pltpu.roll(edge, 1, 1), edge, pltpu.roll(edge, LANES - 1, 1)], axis=0
    ).astype(BF16)


def edge_terms(weights, edge):
    ch = edge.shape[0]
    taps = jnp.dot(weights, stacked_rows(edge), preferred_element_type=F32)
    return jnp.where(lane_of((ch, LANES)) < SIDE, taps[:ch], taps[2 * ch :])


def conv_row(weights, rows3, edges, row, offset):
    ch, width = edges.shape[0], rows3.shape[1]
    taps = jnp.dot(weights, rows3, preferred_element_type=F32)
    at = lane_of((ch, LANES))
    left = jnp.sum(jnp.where(at == row + 2, edges, 0.0), axis=1, keepdims=True)
    right = jnp.sum(jnp.where(at == row + 2 + SIDE, edges, 0.0), axis=1, keepdims=True)
    lane = lane_of((ch, width))
    west = jnp.where(lane == 0, left, pltpu.roll(taps[:ch], 1, 1))
    east = jnp.where(lane == width - 1, right, pltpu.roll(taps[2 * ch :], width - 1, 1))
    return taps[ch : 2 * ch] + west + east + offset


def silu(u):
    return u / (1.0 + jnp.exp(-u))


def main_kernel(
    counts, x_ref, w1_ref, w2_ref, vec_ref, ex_ref,
    hid_ref, mid_ref, up_ref, down_ref,
    flat, x, hf, w1, w2, edges1, edges2, mine, far, own, face,
    row_send, row_recv, lon_send, lon_recv, mp_send, mp_recv, lat_send, lat_recv,
):
    ch, rows, width = x_ref.shape
    n_lat, chunks = counts
    lat = lax.axis_index("lat")
    has_up, has_down = lat > 0, lat < n_lat - 1
    above, below = {"lat": lat - 1}, {"lat": lat + 1}
    beside = {"lon": 1 - lax.axis_index("lon")}
    partner = {"mp": 1 - lax.axis_index("mp")}
    MESH = pl.DeviceIdType.MESH

    barrier = pltpu.get_barrier_semaphore()
    pl.semaphore_signal(barrier, inc=1, device_id=beside, device_id_type=MESH)
    pl.semaphore_signal(barrier, inc=1, device_id=partner, device_id_type=MESH)

    @pl.when(has_up)
    def _():
        pl.semaphore_signal(barrier, inc=1, device_id=above, device_id_type=MESH)

    @pl.when(has_down)
    def _():
        pl.semaphore_signal(barrier, inc=1, device_id=below, device_id_type=MESH)

    for j in range(width // LANES):
        flat[j] = x_ref[:, :, j * LANES : (j + 1) * LANES].astype(F32).reshape(ch * rows, LANES)
    for r in range(rows):
        for j in range(width // LANES):
            x[(r + 2) * ch : (r + 3) * ch, j * LANES : (j + 1) * LANES] = flat.at[j][
                pl.ds(r, ch, stride=rows), :
            ].astype(BF16)

    pl.semaphore_wait(barrier, 2 + has_up.astype(jnp.int32) + has_down.astype(jnp.int32))

    def copy(src, dst, send, recv, where):
        return pltpu.make_async_remote_copy(
            src_ref=src, dst_ref=dst, send_sem=send, recv_sem=recv,
            device_id=where, device_id_type=MESH,
        )

    two = 2 * ch
    to_up = copy(
        x.at[pl.ds(two, two)], x.at[pl.ds((rows + 2) * ch, two)],
        row_send.at[0], row_recv.at[0], above,
    )
    to_down = copy(
        x.at[pl.ds(rows * ch, two)], x.at[pl.ds(0, two)],
        row_send.at[1], row_recv.at[1], below,
    )

    @pl.when(has_up)
    def _():
        to_up.start()

    @pl.when(has_down)
    def _():
        to_down.start()

    at = lane_of((ch, LANES))

    def columns(row_list, n):
        zero = jnp.zeros((ch, LANES), F32)
        sent = [zero, zero, zero]
        kept = [zero, zero]
        if n:
            sent = [mine[0, k * ch : (k + 1) * ch] for k in range(3)]
            kept = [own[k * ch : (k + 1) * ch] for k in range(2)]
        for r in row_list:
            here = pl.ds((r + 2) * ch, ch)
            first = x[here, :LANES].astype(F32)
            last = x[here, width - LANES :].astype(F32)
            left, right = at == r + 2, at == r + 2 + SIDE
            sent[0] = jnp.where(left, last[:, LANES - 2 : LANES - 1], sent[0])
            sent[1] = jnp.where(left, last[:, LANES - 1 :], sent[1])
            sent[1] = jnp.where(right, first[:, :1], sent[1])
            sent[2] = jnp.where(right, first[:, 1:2], sent[2])
            kept[0] = jnp.where(right, last[:, LANES - 1 :], kept[0])
            kept[1] = jnp.where(left, first[:, :1], kept[1])
        for k in range(3):
            mine[n, k * ch : (k + 1) * ch] = sent[k]
        for k in range(2):
            own[k * ch : (k + 1) * ch] = kept[k]
        return copy(mine.at[n], far.at[n], lon_send.at[n], lon_recv.at[n], beside)

    lon0 = columns(range(rows), 0)
    lon0.start()

    def taps(src, dst):
        for c in range(3):
            block = jnp.concatenate([src[a, c].astype(F32) for a in range(3)], axis=0)
            dst[c * ch : (c + 1) * ch] = block.T.astype(BF16)

    taps(w1_ref, w1)
    taps(w2_ref, w2)
    b1, b2, gain = vec_ref[:, 0:1], vec_ref[:, 1:2], vec_ref[:, 2:3]
    lon0.wait()
    edges1[...] = edge_terms(w1[...], far[0, ch : 2 * ch])

    def first(r):
        rows3 = x[pl.ds(pl.multiple_of((r + 1) * ch, 16), 3 * ch), :]
        return silu(conv_row(w1[...], rows3, edges1[...], r, vec_ref[:, 0:1])).astype(BF16)

    split = rows - 4

    @pl.loop(1, split)
    def _(r):
        hf[pl.ds(pl.multiple_of((r + 1) * ch, 16), ch), :] = first(r)

    @pl.when(has_up)
    def _():
        to_up.wait_send()
        to_down.wait_recv()

    @pl.when(has_down)
    def _():
        to_down.wait_send()
        to_up.wait_recv()

    @pl.when(jnp.logical_not(has_up))
    def _():
        x[:two] = jnp.zeros((two, width), BF16)

    @pl.when(jnp.logical_not(has_down))
    def _():
        x[(rows + 2) * ch :] = jnp.zeros((two, width), BF16)

    lon1 = columns((-2, -1, rows, rows + 1), 1)
    lon1.start()

    @pl.loop(split, rows - 1)
    def _(r):
        hf[pl.ds(pl.multiple_of((r + 1) * ch, 16), ch), :] = first(r)

    lon1.wait()
    edges1[...] = edge_terms(w1[...], far[1, ch : 2 * ch])

    @pl.loop(0, 4)
    def _(q):
        r = jnp.where(q < 2, q - 1, rows + q - 3)
        hf[pl.ds(pl.multiple_of((r + 1) * ch, 16), ch), :] = first(r)

    @pl.when(jnp.logical_not(has_up))
    def _():
        hf[:ch] = jnp.zeros((ch, width), BF16)

    @pl.when(jnp.logical_not(has_down))
    def _():
        hf[(rows + 1) * ch :] = jnp.zeros((ch, width), BF16)

    column = None
    for k in range(3):
        edge = far[1, k * ch : (k + 1) * ch]
        if k != 1:
            edge = edge + own[(k // 2) * ch : (k // 2 + 1) * ch]
        term = jnp.dot(
            w1[k * ch : (k + 1) * ch], stacked_rows(edge), preferred_element_type=F32
        )
        column = term if column is None else column + term
    column = silu(column + b1)
    lane = jnp.where(at >= SIDE, at - SIDE, at)
    lowest = jnp.where(has_up, 1, 2)
    highest = jnp.where(has_down, rows + 2, rows + 1)
    column = jnp.where((lane < lowest) | (lane > highest), 0.0, column)
    edges2[...] = edge_terms(w2[...], column.astype(BF16).astype(F32))

    size = rows // chunks
    to_partner = []
    for n in range(chunks):
        part = pl.ds(n * size, size)
        to_partner.append(copy(face.at[part], mid_ref.at[part], mp_send.at[n], mp_recv.at[n], partner))
    face_up, face_down = [], []
    for n in range(chunks):
        part = pl.ds(n * size, size)
        face_up.append(copy(mid_ref.at[part], down_ref.at[part], lat_send.at[0, n], lat_recv.at[0, n], above))
        face_down.append(copy(mid_ref.at[part], up_ref.at[part], lat_send.at[1, n], lat_recv.at[1, n], below))

    def forward(n):
        to_partner[n].wait()

        @pl.when(has_up)
        def _():
            face_up[n].start()

        @pl.when(has_down)
        def _():
            face_down[n].start()

    for n in range(chunks):

        @pl.loop(n * size, (n + 1) * size)
        def _(r):
            here = pl.ds(pl.multiple_of(r * ch, 16), ch)
            rows3 = hf[pl.ds(pl.multiple_of(r * ch, 16), 3 * ch), :]
            u = conv_row(w2[...], rows3, edges2[...], r, vec_ref[:, 1:2])
            u = u + x[pl.ds(pl.multiple_of((r + 2) * ch, 16), ch), :].astype(F32)
            mean = jnp.sum(u * u, axis=0, keepdims=True) * (1.0 / ch)
            h = (u * lax.rsqrt(mean + 1e-06) * vec_ref[:, 2:3]).astype(BF16)
            hid_ref[here, :] = h
            face[r] = jnp.dot(ex_ref[...], h, preferred_element_type=F32).astype(BF16)

        to_partner[n].start()
        if n:
            forward(n - 1)
    forward(chunks - 1)

    @pl.when(has_up)
    def _():
        for n in range(chunks):
            face_up[n].wait_send()
            face_down[n].wait_recv()

    @pl.when(has_down)
    def _():
        for n in range(chunks):
            face_down[n].wait_send()
            face_up[n].wait_recv()

    @pl.when(jnp.logical_not(has_up))
    def _():
        up_ref[...] = jnp.zeros(up_ref.shape, BF16)

    @pl.when(jnp.logical_not(has_down))
    def _():
        down_ref[...] = jnp.zeros(down_ref.shape, BF16)


def third_kernel(
    rows_ref, weights_ref, hid_ref, up_ref, mid_ref, down_ref, im_ref, mask_ref, out_ref, band, flat
):
    ch, step, width = out_ref.shape
    rows = up_ref.shape[0]
    base = pl.program_id(0) * step
    band[:rows] = up_ref[...].astype(F32)
    band[rows : 2 * rows] = mid_ref[...].astype(F32)
    band[2 * rows :] = down_ref[...].astype(F32)
    for d in range(step):
        total = None
        for k in range(rows_ref.shape[1]):
            term = weights_ref[base + d, k] * band[rows_ref[base + d, k]]
            total = term if total is None else total + term
        mixed = jnp.dot(im_ref[...], total.astype(BF16), preferred_element_type=F32)
        h = hid_ref[d * ch : (d + 1) * ch, :].astype(F32)
        value = h + mask_ref[d : d + 1, :].astype(F32) * mixed
        for j in range(width // LANES):
            flat.at[j][pl.ds(d, ch, stride=step), :] = value[:, j * LANES : (j + 1) * LANES]
    for j in range(width // LANES):
        out_ref[:, :, j * LANES : (j + 1) * LANES] = (
            flat[j].reshape(ch, step, LANES).astype(BF16)
        )


def vmem():
    return pl.BlockSpec(memory_space=pltpu.VMEM)


def smem():
    return pl.BlockSpec(memory_space=pltpu.SMEM)


def params():
    return pltpu.CompilerParams(vmem_limit_bytes=VMEM_LIMIT)


def on_device(
    state, conv_first, bias_first, conv_second, bias_second, norm_gain, export_weight,
    import_weight, regrid_rows, regrid_weights, sea_mask,
):
    source = state[0]
    ch, rows, width = source.shape
    lat = lax.axis_index("lat")
    n_lat = lax.axis_size("lat")

    vectors = jnp.stack([bias_first[0], bias_second[0], norm_gain[0]], axis=1)
    n_face = export_weight.shape[2]
    chunks = 4
    fields = jax.ShapeDtypeStruct((rows, n_face, width), BF16)
    dma = pltpu.SemaphoreType.DMA
    hidden, mid, up, down = pl.pallas_call(
        functools.partial(main_kernel, (n_lat, chunks)),
        name="convolutions",
        out_shape=(jax.ShapeDtypeStruct((rows * ch, width), BF16), fields, fields, fields),
        in_specs=[vmem()] * 5,
        out_specs=(vmem(),) * 4,
        scratch_shapes=[
            pltpu.VMEM((width // LANES, rows * ch, LANES), F32),
            pltpu.VMEM(((rows + 4) * ch, width), BF16),
            pltpu.VMEM(((rows + 2) * ch, width), BF16),
            pltpu.VMEM((3 * ch, 3 * ch), BF16),
            pltpu.VMEM((3 * ch, 3 * ch), BF16),
            pltpu.VMEM((ch, LANES), F32),
            pltpu.VMEM((ch, LANES), F32),
            pltpu.VMEM((2, 3 * ch, LANES), F32),
            pltpu.VMEM((2, 3 * ch, LANES), F32),
            pltpu.VMEM((2 * ch, LANES), F32),
            pltpu.VMEM((rows, n_face, width), BF16),
            dma((2,)), dma((2,)), dma((2,)), dma((2,)),
            dma((chunks,)), dma((chunks,)), dma((2, chunks)), dma((2, chunks)),
        ],
        compiler_params=pltpu.CompilerParams(
            vmem_limit_bytes=VMEM_LIMIT, collective_id=0, has_side_effects=True
        ),
    )(source, conv_first[0], conv_second[0], vectors, export_weight[0].T)

    weights = regrid_weights[0]
    normed = weights / jnp.sum(weights, axis=1, keepdims=True)
    local_rows = regrid_rows[0] - (lat - 1) * rows

    step = 8
    whole = lambda shape: pl.BlockSpec(shape, lambda i: (0,) * len(shape))
    out = pl.pallas_call(
        third_kernel,
        name="exchange",
        grid=(rows // step,),
        out_shape=jax.ShapeDtypeStruct((ch, rows, width), BF16),
        in_specs=[
            smem(),
            smem(),
            pl.BlockSpec((step * ch, width), lambda i: (i, 0)),
            whole(mid.shape),
            whole(mid.shape),
            whole(mid.shape),
            whole((ch, n_face)),
            pl.BlockSpec((step, width), lambda i: (i, 0)),
        ],
        out_specs=pl.BlockSpec((ch, step, width), lambda i: (0, i, 0)),
        scratch_shapes=[
            pltpu.VMEM((3 * rows, n_face, width), F32),
            pltpu.VMEM((width // LANES, step * ch, LANES), F32),
        ],
        compiler_params=params(),
    )(local_rows, normed, hidden, up, mid, down, import_weight[0].T, sea_mask[0])
    return out[None]


def solution(mesh):
    return jax.shard_map(
        on_device,
        mesh=mesh,
        in_specs=(
            P("mp", None, "lat", "lon"),
            P("mp", None, None, None, None),
            P("mp", None),
            P("mp", None, None, None, None),
            P("mp", None),
            P("mp", None),
            P("mp", None, None),
            P("mp", None, None),
            P("mp", "lat", None),
            P("mp", "lat", None),
            P("mp", "lat", "lon"),
        ),
        out_specs=P("mp", None, "lat", "lon"),
        check_vma=False,
    )
```

```python
import functools

import jax
import jax.numpy as jnp
from jax import lax
from jax.experimental import pallas as pl
from jax.experimental.pallas import tpu as pltpu
from jax.sharding import PartitionSpec as P

F32 = jnp.float32
BF16 = jnp.bfloat16
LANES = 128
SIDE = 64
VMEM_LIMIT = 58 * 1024 * 1024


def lane_of(shape):
    return lax.broadcasted_iota(jnp.int32, shape, 1)


def stacked_rows(edge):
    return jnp.concatenate(
        [pltpu.roll(edge, 1, 1), edge, pltpu.roll(edge, LANES - 1, 1)], axis=0
    ).astype(BF16)


def edge_terms(weights, edge):
    ch = edge.shape[0]
    taps = jnp.dot(weights, stacked_rows(edge), preferred_element_type=F32)
    return jnp.where(lane_of((ch, LANES)) < SIDE, taps[:ch], taps[2 * ch :])


def conv_row(weights, rows3, edges, row, offset):
    ch, width = edges.shape[0], rows3.shape[1]
    taps = jnp.dot(weights, rows3, preferred_element_type=F32)
    lane = lane_of((ch, LANES))
    left = pltpu.roll(edges, LANES - 2 - row, 1)
    right = pltpu.roll(edges, LANES - 1 - (row + 2 + SIDE), 1)
    west = pltpu.roll(taps[:ch], 1, 1)
    west = jnp.concatenate([jnp.where(lane == 0, left, west[:, :LANES]), west[:, LANES:]], axis=1)
    east = pltpu.roll(taps[2 * ch :], width - 1, 1)
    east = jnp.concatenate(
        [east[:, : width - LANES], jnp.where(lane == LANES - 1, right, east[:, width - LANES :])],
        axis=1,
    )
    return taps[ch : 2 * ch] + west + east + offset


def silu(u):
    half = 0.5 * u
    return half + half * jnp.tanh(half)


def main_kernel(
    counts, x_ref, w1_ref, w2_ref, vec_ref, ex_ref,
    hid_ref, mid_ref, up_ref, down_ref,
    flat, x, hf, w1, w2, edges1, edges2, mine, far, own, face,
    row_send, row_recv, lon_send, lon_recv, mp_send, mp_recv, lat_send, lat_recv,
):
    ch, rows, width = x_ref.shape
    n_lat, chunks = counts
    lat = lax.axis_index("lat")
    has_up, has_down = lat > 0, lat < n_lat - 1
    above, below = {"lat": lat - 1}, {"lat": lat + 1}
    beside = {"lon": 1 - lax.axis_index("lon")}
    partner = {"mp": 1 - lax.axis_index("mp")}
    MESH = pl.DeviceIdType.MESH

    barrier = pltpu.get_barrier_semaphore()
    pl.semaphore_signal(barrier, inc=1, device_id=beside, device_id_type=MESH)
    pl.semaphore_signal(barrier, inc=1, device_id=partner, device_id_type=MESH)

    @pl.when(has_up)
    def _():
        pl.semaphore_signal(barrier, inc=1, device_id=above, device_id_type=MESH)

    @pl.when(has_down)
    def _():
        pl.semaphore_signal(barrier, inc=1, device_id=below, device_id_type=MESH)

    for j in range(width // LANES):
        flat[j] = x_ref[:, :, j * LANES : (j + 1) * LANES].astype(F32).reshape(ch * rows, LANES)
    for r in range(rows):
        for j in range(width // LANES):
            x[(r + 2) * ch : (r + 3) * ch, j * LANES : (j + 1) * LANES] = flat.at[j][
                pl.ds(r, ch, stride=rows), :
            ].astype(BF16)

    pl.semaphore_wait(barrier, 2 + has_up.astype(jnp.int32) + has_down.astype(jnp.int32))

    def copy(src, dst, send, recv, where):
        return pltpu.make_async_remote_copy(
            src_ref=src, dst_ref=dst, send_sem=send, recv_sem=recv,
            device_id=where, device_id_type=MESH,
        )

    two = 2 * ch
    to_up = copy(
        x.at[pl.ds(two, two)], x.at[pl.ds((rows + 2) * ch, two)],
        row_send.at[0], row_recv.at[0], above,
    )
    to_down = copy(
        x.at[pl.ds(rows * ch, two)], x.at[pl.ds(0, two)],
        row_send.at[1], row_recv.at[1], below,
    )

    @pl.when(has_up)
    def _():
        to_up.start()

    @pl.when(has_down)
    def _():
        to_down.start()

    at = lane_of((ch, LANES))

    def columns(row_list, n):
        zero = jnp.zeros((ch, LANES), F32)
        sent = [zero, zero, zero]
        kept = [zero, zero]
        if n:
            sent = [mine[0, k * ch : (k + 1) * ch] for k in range(3)]
            kept = [own[k * ch : (k + 1) * ch] for k in range(2)]
        for r in row_list:
            here = pl.ds((r + 2) * ch, ch)
            first = x[here, :LANES].astype(F32)
            last = x[here, width - LANES :].astype(F32)
            left, right = at == r + 2, at == r + 2 + SIDE
            sent[0] = jnp.where(left, last[:, LANES - 2 : LANES - 1], sent[0])
            sent[1] = jnp.where(left, last[:, LANES - 1 :], sent[1])
            sent[1] = jnp.where(right, first[:, :1], sent[1])
            sent[2] = jnp.where(right, first[:, 1:2], sent[2])
            kept[0] = jnp.where(right, last[:, LANES - 1 :], kept[0])
            kept[1] = jnp.where(left, first[:, :1], kept[1])
        for k in range(3):
            mine[n, k * ch : (k + 1) * ch] = sent[k]
        for k in range(2):
            own[k * ch : (k + 1) * ch] = kept[k]
        return copy(mine.at[n], far.at[n], lon_send.at[n], lon_recv.at[n], beside)

    lon0 = columns(range(rows), 0)
    lon0.start()

    def taps(src, dst):
        for c in range(3):
            block = jnp.concatenate([src[a, c].astype(F32) for a in range(3)], axis=0)
            dst[c * ch : (c + 1) * ch] = block.T.astype(BF16)

    taps(w1_ref, w1)
    taps(w2_ref, w2)
    b1, b2, gain = vec_ref[:, 0:1], vec_ref[:, 1:2], vec_ref[:, 2:3]
    lon0.wait()
    edges1[...] = edge_terms(w1[...], far[0, ch : 2 * ch])

    def first(r):
        rows3 = x[pl.ds(pl.multiple_of((r + 1) * ch, 16), 3 * ch), :]
        return silu(conv_row(w1[...], rows3, edges1[...], r, vec_ref[:, 0:1])).astype(BF16)

    @pl.loop(1, rows - 1)
    def _(r):
        hf[pl.ds(pl.multiple_of((r + 1) * ch, 16), ch), :] = first(r)

    def column_terms(n):
        column = None
        for k in range(3):
            edge = far[n, k * ch : (k + 1) * ch]
            if k != 1:
                edge = edge + own[(k // 2) * ch : (k // 2 + 1) * ch]
            term = jnp.dot(
                w1[k * ch : (k + 1) * ch], stacked_rows(edge), preferred_element_type=F32
            )
            column = term if column is None else column + term
        column = silu(column + b1)
        lane = jnp.where(at >= SIDE, at - SIDE, at)
        lowest = jnp.where(has_up, 1, 2)
        highest = jnp.where(has_down, rows + 2, rows + 1)
        column = jnp.where((lane < lowest) | (lane > highest), 0.0, column)
        edges2[...] = edge_terms(w2[...], column.astype(BF16).astype(F32))

    third = (rows - 4) // 3
    parts = [(2 + n * third, third) for n in range(3)] + [(0, 2), (rows - 2, 2)]
    to_partner = []
    for n in range(chunks):
        part = pl.ds(*parts[n])
        to_partner.append(copy(face.at[part], mid_ref.at[part], mp_send.at[n], mp_recv.at[n], partner))
    face_up, face_down = [], []
    for n in range(chunks):
        part = pl.ds(*parts[n])
        face_up.append(copy(mid_ref.at[part], down_ref.at[part], lat_send.at[0, n], lat_recv.at[0, n], above))
        face_down.append(copy(mid_ref.at[part], up_ref.at[part], lat_send.at[1, n], lat_recv.at[1, n], below))

    def forward(n):
        to_partner[n].wait()

        @pl.when(has_up)
        def _():
            face_up[n].start()

        @pl.when(has_down)
        def _():
            face_down[n].start()

    def finish(n):
        @pl.loop(parts[n][0], sum(parts[n]))
        def _(r):
            here = pl.ds(pl.multiple_of(r * ch, 16), ch)
            rows3 = hf[pl.ds(pl.multiple_of(r * ch, 16), 3 * ch), :]
            u = conv_row(w2[...], rows3, edges2[...], r, vec_ref[:, 1:2])
            u = u + x[pl.ds(pl.multiple_of((r + 2) * ch, 16), ch), :].astype(F32)
            mean = jnp.sum(u * u, axis=0, keepdims=True) * (1.0 / ch)
            h = (u * lax.rsqrt(mean + 1e-06) * vec_ref[:, 2:3]).astype(BF16)
            hid_ref[here, :] = h
            face[r] = jnp.dot(ex_ref[...], h, preferred_element_type=F32).astype(BF16)

        to_partner[n].start()

    column_terms(0)
    finish(0)
    finish(1)
    forward(0)
    finish(2)
    forward(1)

    @pl.when(has_up)
    def _():
        to_up.wait_send()
        to_down.wait_recv()

    @pl.when(has_down)
    def _():
        to_down.wait_send()
        to_up.wait_recv()

    @pl.when(jnp.logical_not(has_up))
    def _():
        x[:two] = jnp.zeros((two, width), BF16)

    @pl.when(jnp.logical_not(has_down))
    def _():
        x[(rows + 2) * ch :] = jnp.zeros((two, width), BF16)

    lon1 = columns((-2, -1, rows, rows + 1), 1)
    lon1.start()
    forward(2)
    lon1.wait()
    edges1[...] = edge_terms(w1[...], far[1, ch : 2 * ch])

    @pl.loop(0, 4)
    def _(q):
        r = jnp.where(q < 2, q - 1, rows + q - 3)
        hf[pl.ds(pl.multiple_of((r + 1) * ch, 16), ch), :] = first(r)

    @pl.when(jnp.logical_not(has_up))
    def _():
        hf[:ch] = jnp.zeros((ch, width), BF16)

    @pl.when(jnp.logical_not(has_down))
    def _():
        hf[(rows + 1) * ch :] = jnp.zeros((ch, width), BF16)

    column_terms(1)
    finish(3)
    finish(4)
    forward(3)
    forward(4)

    @pl.when(has_up)
    def _():
        for n in range(chunks):
            face_up[n].wait_send()
            face_down[n].wait_recv()

    @pl.when(has_down)
    def _():
        for n in range(chunks):
            face_down[n].wait_send()
            face_up[n].wait_recv()

    @pl.when(jnp.logical_not(has_up))
    def _():
        up_ref[...] = jnp.zeros(up_ref.shape, BF16)

    @pl.when(jnp.logical_not(has_down))
    def _():
        down_ref[...] = jnp.zeros(down_ref.shape, BF16)


def third_kernel(
    rows_ref, weights_ref, hid_ref, up_ref, mid_ref, down_ref, im_ref, mask_ref, out_ref, band, flat
):
    ch, step, width = out_ref.shape
    rows = up_ref.shape[0]
    base = pl.program_id(0) * step
    start = (lax.axis_index("lat") - 1) * rows
    band[:rows] = up_ref[...].astype(F32)
    band[rows : 2 * rows] = mid_ref[...].astype(F32)
    band[2 * rows :] = down_ref[...].astype(F32)
    for d in range(step):
        total = None
        for k in range(rows_ref.shape[1]):
            weight = weights_ref[base + d, k]
            at = jnp.clip(rows_ref[base + d, k] - start, 0, 3 * rows - 1)
            term = weight * band[at]
            total = term if total is None else total + term
            weight_sum = weight if k == 0 else weight_sum + weight
        total = total / jnp.full(total.shape, weight_sum, F32)
        mixed = jnp.dot(im_ref[...], total.astype(BF16), preferred_element_type=F32)
        h = hid_ref[d * ch : (d + 1) * ch, :].astype(F32)
        value = h + mask_ref[d : d + 1, :].astype(F32) * mixed
        for j in range(width // LANES):
            flat.at[j][pl.ds(d, ch, stride=step), :] = value[:, j * LANES : (j + 1) * LANES]
    for j in range(width // LANES):
        out_ref[:, :, j * LANES : (j + 1) * LANES] = (
            flat[j].reshape(ch, step, LANES).astype(BF16)
        )


def vmem():
    return pl.BlockSpec(memory_space=pltpu.VMEM)


def smem():
    return pl.BlockSpec(memory_space=pltpu.SMEM)


def params():
    return pltpu.CompilerParams(vmem_limit_bytes=VMEM_LIMIT)


def on_device(
    state, conv_first, bias_first, conv_second, bias_second, norm_gain, export_weight,
    import_weight, regrid_rows, regrid_weights, sea_mask,
):
    source = state[0]
    ch, rows, width = source.shape
    n_lat = lax.axis_size("lat")

    vectors = jnp.stack([bias_first[0], bias_second[0], norm_gain[0]], axis=1)
    n_face = export_weight.shape[2]
    chunks = 5
    fields = jax.ShapeDtypeStruct((rows, n_face, width), BF16)
    dma = pltpu.SemaphoreType.DMA
    hidden, mid, up, down = pl.pallas_call(
        functools.partial(main_kernel, (n_lat, chunks)),
        name="convolutions",
        out_shape=(jax.ShapeDtypeStruct((rows * ch, width), BF16), fields, fields, fields),
        in_specs=[vmem()] * 5,
        out_specs=(vmem(),) * 4,
        scratch_shapes=[
            pltpu.VMEM((width // LANES, rows * ch, LANES), F32),
            pltpu.VMEM(((rows + 4) * ch, width), BF16),
            pltpu.VMEM(((rows + 2) * ch, width), BF16),
            pltpu.VMEM((3 * ch, 3 * ch), BF16),
            pltpu.VMEM((3 * ch, 3 * ch), BF16),
            pltpu.VMEM((ch, LANES), F32),
            pltpu.VMEM((ch, LANES), F32),
            pltpu.VMEM((2, 3 * ch, LANES), F32),
            pltpu.VMEM((2, 3 * ch, LANES), F32),
            pltpu.VMEM((2 * ch, LANES), F32),
            pltpu.VMEM((rows, n_face, width), BF16),
            dma((2,)), dma((2,)), dma((2,)), dma((2,)),
            dma((chunks,)), dma((chunks,)), dma((2, chunks)), dma((2, chunks)),
        ],
        compiler_params=pltpu.CompilerParams(
            vmem_limit_bytes=VMEM_LIMIT, collective_id=0, has_side_effects=True
        ),
    )(source, conv_first[0], conv_second[0], vectors, export_weight[0].T)

    step = 8
    whole = lambda shape: pl.BlockSpec(shape, lambda i: (0,) * len(shape))
    out = pl.pallas_call(
        third_kernel,
        name="exchange",
        grid=(rows // step,),
        out_shape=jax.ShapeDtypeStruct((ch, rows, width), BF16),
        in_specs=[
            smem(),
            smem(),
            pl.BlockSpec((step * ch, width), lambda i: (i, 0)),
            whole(mid.shape),
            whole(mid.shape),
            whole(mid.shape),
            whole((ch, n_face)),
            pl.BlockSpec((step, width), lambda i: (i, 0)),
        ],
        out_specs=pl.BlockSpec((ch, step, width), lambda i: (0, i, 0)),
        scratch_shapes=[
            pltpu.VMEM((3 * rows, n_face, width), F32),
            pltpu.VMEM((width // LANES, step * ch, LANES), F32),
        ],
        compiler_params=params(),
    )(regrid_rows[0], regrid_weights[0], hidden, up, mid, down, import_weight[0].T, sea_mask[0])
    return out[None]


def solution(mesh):
    return jax.shard_map(
        on_device,
        mesh=mesh,
        in_specs=(
            P("mp", None, "lat", "lon"),
            P("mp", None, None, None, None),
            P("mp", None),
            P("mp", None, None, None, None),
            P("mp", None),
            P("mp", None),
            P("mp", None, None),
            P("mp", None, None),
            P("mp", "lat", None),
            P("mp", "lat", None),
            P("mp", "lat", "lon"),
        ),
        out_specs=P("mp", None, "lat", "lon"),
        check_vma=False,
    )
```

```python
import functools

import jax
import jax.numpy as jnp
from jax import lax
from jax.experimental import pallas as pl
from jax.experimental.pallas import tpu as pltpu
from jax.sharding import PartitionSpec as P

F32 = jnp.float32
BF16 = jnp.bfloat16
LANES = 128
SIDE = 64
VMEM_LIMIT = 58 * 1024 * 1024


def lane_of(shape):
    return lax.broadcasted_iota(jnp.int32, shape, 1)


def stacked_rows(edge):
    return jnp.concatenate(
        [pltpu.roll(edge, 1, 1), edge, pltpu.roll(edge, LANES - 1, 1)], axis=0
    ).astype(BF16)


def edge_terms(weights, edge):
    ch = edge.shape[0]
    taps = jnp.dot(weights, stacked_rows(edge), preferred_element_type=F32)
    return jnp.where(lane_of((ch, LANES)) < SIDE, taps[:ch], taps[2 * ch :])


def conv_row(weights, rows3, edges, row, offset):
    ch, width = edges.shape[0], rows3.shape[1]
    taps = jnp.dot(weights, rows3, preferred_element_type=F32)
    lane = lane_of((ch, LANES))
    left = pltpu.roll(edges, LANES - 2 - row, 1)
    right = pltpu.roll(edges, LANES - 1 - (row + 2 + SIDE), 1)
    west = pltpu.roll(taps[:ch], 1, 1)
    west = jnp.concatenate([jnp.where(lane == 0, left, west[:, :LANES]), west[:, LANES:]], axis=1)
    east = pltpu.roll(taps[2 * ch :], width - 1, 1)
    east = jnp.concatenate(
        [east[:, : width - LANES], jnp.where(lane == LANES - 1, right, east[:, width - LANES :])],
        axis=1,
    )
    return taps[ch : 2 * ch] + west + east + offset


def silu(u):
    half = 0.5 * u
    return half + half * jnp.tanh(half)


def main_kernel(
    counts, x_ref, w1_ref, w2_ref, vec_ref, ex_ref,
    hid_ref, mid_ref, up_ref, down_ref,
    flat, x, hf, w1, w2, edges1, edges2, mine, far, own, face,
    row_send, row_recv, lon_send, lon_recv, mp_send, mp_recv, lat_send, lat_recv,
):
    ch, rows, width = x_ref.shape
    n_lat, chunks = counts
    lat = lax.axis_index("lat")
    has_up, has_down = lat > 0, lat < n_lat - 1
    above, below = {"lat": lat - 1}, {"lat": lat + 1}
    beside = {"lon": 1 - lax.axis_index("lon")}
    partner = {"mp": 1 - lax.axis_index("mp")}
    MESH = pl.DeviceIdType.MESH

    barrier = pltpu.get_barrier_semaphore()
    pl.semaphore_signal(barrier, inc=1, device_id=beside, device_id_type=MESH)
    pl.semaphore_signal(barrier, inc=1, device_id=partner, device_id_type=MESH)

    @pl.when(has_up)
    def _():
        pl.semaphore_signal(barrier, inc=1, device_id=above, device_id_type=MESH)

    @pl.when(has_down)
    def _():
        pl.semaphore_signal(barrier, inc=1, device_id=below, device_id_type=MESH)

    for j in range(width // LANES):
        flat[j] = x_ref[:, :, j * LANES : (j + 1) * LANES].astype(F32).reshape(ch * rows, LANES)
    def lay_out(row_list):
        for r in row_list:
            for j in range(width // LANES):
                x[(r + 2) * ch : (r + 3) * ch, j * LANES : (j + 1) * LANES] = flat.at[j][
                    pl.ds(r, ch, stride=rows), :
                ].astype(BF16)

    lay_out((0, 1, rows - 2, rows - 1))
    pl.semaphore_wait(barrier, 2 + has_up.astype(jnp.int32) + has_down.astype(jnp.int32))

    def copy(src, dst, send, recv, where):
        return pltpu.make_async_remote_copy(
            src_ref=src, dst_ref=dst, send_sem=send, recv_sem=recv,
            device_id=where, device_id_type=MESH,
        )

    two = 2 * ch
    to_up = copy(
        x.at[pl.ds(two, two)], x.at[pl.ds((rows + 2) * ch, two)],
        row_send.at[0], row_recv.at[0], above,
    )
    to_down = copy(
        x.at[pl.ds(rows * ch, two)], x.at[pl.ds(0, two)],
        row_send.at[1], row_recv.at[1], below,
    )

    @pl.when(has_up)
    def _():
        to_up.start()

    @pl.when(has_down)
    def _():
        to_down.start()

    lay_out(range(2, rows - 2))
    at = lane_of((ch, LANES))

    def columns(row_list, n):
        zero = jnp.zeros((ch, LANES), F32)
        sent = [zero, zero, zero]
        kept = [zero, zero]
        if n:
            sent = [mine[0, k * ch : (k + 1) * ch] for k in range(3)]
            kept = [own[k * ch : (k + 1) * ch] for k in range(2)]
        for r in row_list:
            here = pl.ds((r + 2) * ch, ch)
            first = x[here, :LANES].astype(F32)
            last = x[here, width - LANES :].astype(F32)
            left, right = at == r + 2, at == r + 2 + SIDE
            sent[0] = jnp.where(left, last[:, LANES - 2 : LANES - 1], sent[0])
            sent[1] = jnp.where(left, last[:, LANES - 1 :], sent[1])
            sent[1] = jnp.where(right, first[:, :1], sent[1])
            sent[2] = jnp.where(right, first[:, 1:2], sent[2])
            kept[0] = jnp.where(right, last[:, LANES - 1 :], kept[0])
            kept[1] = jnp.where(left, first[:, :1], kept[1])
        for k in range(3):
            mine[n, k * ch : (k + 1) * ch] = sent[k]
        for k in range(2):
            own[k * ch : (k + 1) * ch] = kept[k]
        return copy(mine.at[n], far.at[n], lon_send.at[n], lon_recv.at[n], beside)

    lon0 = columns(range(rows), 0)
    lon0.start()

    def taps(src, dst):
        for c in range(3):
            block = jnp.concatenate([src[a, c].astype(F32) for a in range(3)], axis=0)
            dst[c * ch : (c + 1) * ch] = block.T.astype(BF16)

    taps(w1_ref, w1)
    taps(w2_ref, w2)
    b1, b2, gain = vec_ref[:, 0:1], vec_ref[:, 1:2], vec_ref[:, 2:3]
    lon0.wait()
    edges1[...] = edge_terms(w1[...], far[0, ch : 2 * ch])

    def first(r):
        rows3 = x[pl.ds(pl.multiple_of((r + 1) * ch, 16), 3 * ch), :]
        return silu(conv_row(w1[...], rows3, edges1[...], r, vec_ref[:, 0:1])).astype(BF16)

    @pl.loop(1, rows - 1)
    def _(r):
        hf[pl.ds(pl.multiple_of((r + 1) * ch, 16), ch), :] = first(r)

    def column_terms(n):
        column = None
        for k in range(3):
            edge = far[n, k * ch : (k + 1) * ch]
            if k != 1:
                edge = edge + own[(k // 2) * ch : (k // 2 + 1) * ch]
            term = jnp.dot(
                w1[k * ch : (k + 1) * ch], stacked_rows(edge), preferred_element_type=F32
            )
            column = term if column is None else column + term
        column = silu(column + b1)
        lane = jnp.where(at >= SIDE, at - SIDE, at)
        lowest = jnp.where(has_up, 1, 2)
        highest = jnp.where(has_down, rows + 2, rows + 1)
        column = jnp.where((lane < lowest) | (lane > highest), 0.0, column)
        edges2[...] = edge_terms(w2[...], column.astype(BF16).astype(F32))

    third = (rows - 4) // 3
    parts = [(2 + n * third, third) for n in range(3)] + [(0, 2), (rows - 2, 2)]
    to_partner = []
    for n in range(chunks):
        part = pl.ds(*parts[n])
        to_partner.append(copy(face.at[part], mid_ref.at[part], mp_send.at[n], mp_recv.at[n], partner))
    face_up, face_down = [], []
    for n in range(chunks):
        part = pl.ds(*parts[n])
        face_up.append(copy(mid_ref.at[part], down_ref.at[part], lat_send.at[0, n], lat_recv.at[0, n], above))
        face_down.append(copy(mid_ref.at[part], up_ref.at[part], lat_send.at[1, n], lat_recv.at[1, n], below))

    def forward(n):
        to_partner[n].wait()

        @pl.when(has_up)
        def _():
            face_up[n].start()

        @pl.when(has_down)
        def _():
            face_down[n].start()

    def finish(n):
        @pl.loop(parts[n][0], sum(parts[n]))
        def _(r):
            here = pl.ds(pl.multiple_of(r * ch, 16), ch)
            rows3 = hf[pl.ds(pl.multiple_of(r * ch, 16), 3 * ch), :]
            u = conv_row(w2[...], rows3, edges2[...], r, vec_ref[:, 1:2])
            u = u + x[pl.ds(pl.multiple_of((r + 2) * ch, 16), ch), :].astype(F32)
            mean = jnp.sum(u * u, axis=0, keepdims=True) * (1.0 / ch)
            h = (u * lax.rsqrt(mean + 1e-06) * vec_ref[:, 2:3]).astype(BF16)
            hid_ref[here, :] = h
            face[r] = jnp.dot(ex_ref[...], h, preferred_element_type=F32).astype(BF16)

        to_partner[n].start()

    column_terms(0)
    finish(0)
    finish(1)
    forward(0)
    finish(2)
    forward(1)

    @pl.when(has_up)
    def _():
        to_up.wait_send()
        to_down.wait_recv()

    @pl.when(has_down)
    def _():
        to_down.wait_send()
        to_up.wait_recv()

    @pl.when(jnp.logical_not(has_up))
    def _():
        x[:two] = jnp.zeros((two, width), BF16)

    @pl.when(jnp.logical_not(has_down))
    def _():
        x[(rows + 2) * ch :] = jnp.zeros((two, width), BF16)

    lon1 = columns((-2, -1, rows, rows + 1), 1)
    lon1.start()
    forward(2)
    lon1.wait()
    edges1[...] = edge_terms(w1[...], far[1, ch : 2 * ch])

    @pl.loop(0, 4)
    def _(q):
        r = jnp.where(q < 2, q - 1, rows + q - 3)
        hf[pl.ds(pl.multiple_of((r + 1) * ch, 16), ch), :] = first(r)

    @pl.when(jnp.logical_not(has_up))
    def _():
        hf[:ch] = jnp.zeros((ch, width), BF16)

    @pl.when(jnp.logical_not(has_down))
    def _():
        hf[(rows + 1) * ch :] = jnp.zeros((ch, width), BF16)

    column_terms(1)
    finish(3)
    finish(4)
    forward(3)
    forward(4)

    @pl.when(has_up)
    def _():
        for n in range(chunks):
            face_up[n].wait_send()
            face_down[n].wait_recv()

    @pl.when(has_down)
    def _():
        for n in range(chunks):
            face_down[n].wait_send()
            face_up[n].wait_recv()

    @pl.when(jnp.logical_not(has_up))
    def _():
        up_ref[...] = jnp.zeros(up_ref.shape, BF16)

    @pl.when(jnp.logical_not(has_down))
    def _():
        down_ref[...] = jnp.zeros(down_ref.shape, BF16)


def third_kernel(
    rows_ref, weights_ref, hid_ref, up_ref, mid_ref, down_ref, im_ref, mask_ref, out_ref, band, flat
):
    ch, step, width = out_ref.shape
    rows = up_ref.shape[0]
    base = pl.program_id(0) * step
    start = (lax.axis_index("lat") - 1) * rows
    band[:rows] = up_ref[...].astype(F32)
    band[rows : 2 * rows] = mid_ref[...].astype(F32)
    band[2 * rows :] = down_ref[...].astype(F32)
    for d in range(step):
        total = None
        for k in range(rows_ref.shape[1]):
            weight = weights_ref[base + d, k]
            at = jnp.clip(rows_ref[base + d, k] - start, 0, 3 * rows - 1)
            term = weight * band[at]
            total = term if total is None else total + term
            weight_sum = weight if k == 0 else weight_sum + weight
        total = total / jnp.full(total.shape, weight_sum, F32)
        mixed = jnp.dot(im_ref[...], total.astype(BF16), preferred_element_type=F32)
        h = hid_ref[d * ch : (d + 1) * ch, :].astype(F32)
        value = h + mask_ref[d : d + 1, :].astype(F32) * mixed
        for j in range(width // LANES):
            flat.at[j][pl.ds(d, ch, stride=step), :] = value[:, j * LANES : (j + 1) * LANES]
    for j in range(width // LANES):
        out_ref[:, :, j * LANES : (j + 1) * LANES] = (
            flat[j].reshape(ch, step, LANES).astype(BF16)
        )


def vmem():
    return pl.BlockSpec(memory_space=pltpu.VMEM)


def smem():
    return pl.BlockSpec(memory_space=pltpu.SMEM)


def params():
    return pltpu.CompilerParams(vmem_limit_bytes=VMEM_LIMIT)


def on_device(
    state, conv_first, bias_first, conv_second, bias_second, norm_gain, export_weight,
    import_weight, regrid_rows, regrid_weights, sea_mask,
):
    source = state[0]
    ch, rows, width = source.shape
    n_lat = lax.axis_size("lat")

    vectors = jnp.stack([bias_first[0], bias_second[0], norm_gain[0]], axis=1)
    n_face = export_weight.shape[2]
    chunks = 5
    fields = jax.ShapeDtypeStruct((rows, n_face, width), BF16)
    dma = pltpu.SemaphoreType.DMA
    hidden, mid, up, down = pl.pallas_call(
        functools.partial(main_kernel, (n_lat, chunks)),
        name="convolutions",
        out_shape=(jax.ShapeDtypeStruct((rows * ch, width), BF16), fields, fields, fields),
        in_specs=[vmem()] * 5,
        out_specs=(vmem(),) * 4,
        scratch_shapes=[
            pltpu.VMEM((width // LANES, rows * ch, LANES), F32),
            pltpu.VMEM(((rows + 4) * ch, width), BF16),
            pltpu.VMEM(((rows + 2) * ch, width), BF16),
            pltpu.VMEM((3 * ch, 3 * ch), BF16),
            pltpu.VMEM((3 * ch, 3 * ch), BF16),
            pltpu.VMEM((ch, LANES), F32),
            pltpu.VMEM((ch, LANES), F32),
            pltpu.VMEM((2, 3 * ch, LANES), F32),
            pltpu.VMEM((2, 3 * ch, LANES), F32),
            pltpu.VMEM((2 * ch, LANES), F32),
            pltpu.VMEM((rows, n_face, width), BF16),
            dma((2,)), dma((2,)), dma((2,)), dma((2,)),
            dma((chunks,)), dma((chunks,)), dma((2, chunks)), dma((2, chunks)),
        ],
        compiler_params=pltpu.CompilerParams(
            vmem_limit_bytes=VMEM_LIMIT, collective_id=0, has_side_effects=True
        ),
    )(source, conv_first[0], conv_second[0], vectors, export_weight[0].T)

    step = 8
    whole = lambda shape: pl.BlockSpec(shape, lambda i: (0,) * len(shape))
    out = pl.pallas_call(
        third_kernel,
        name="exchange",
        grid=(rows // step,),
        out_shape=jax.ShapeDtypeStruct((ch, rows, width), BF16),
        in_specs=[
            smem(),
            smem(),
            pl.BlockSpec((step * ch, width), lambda i: (i, 0)),
            whole(mid.shape),
            whole(mid.shape),
            whole(mid.shape),
            whole((ch, n_face)),
            pl.BlockSpec((step, width), lambda i: (i, 0)),
        ],
        out_specs=pl.BlockSpec((ch, step, width), lambda i: (0, i, 0)),
        scratch_shapes=[
            pltpu.VMEM((3 * rows, n_face, width), F32),
            pltpu.VMEM((width // LANES, step * ch, LANES), F32),
        ],
        compiler_params=params(),
    )(regrid_rows[0], regrid_weights[0], hidden, up, mid, down, import_weight[0].T, sea_mask[0])
    return out[None]


def solution(mesh):
    return jax.shard_map(
        on_device,
        mesh=mesh,
        in_specs=(
            P("mp", None, "lat", "lon"),
            P("mp", None, None, None, None),
            P("mp", None),
            P("mp", None, None, None, None),
            P("mp", None),
            P("mp", None),
            P("mp", None, None),
            P("mp", None, None),
            P("mp", "lat", None),
            P("mp", "lat", None),
            P("mp", "lat", "lon"),
        ),
        out_specs=P("mp", None, "lat", "lon"),
        check_vma=False,
    )
```
